256 devices in a mesh: pair: 64 (over z, y, core), rep: 4 (over x).
Axes of the slice: x: 4, y: 4, z: 8, core: 2. Of those that a mesh axis runs over, the one named last changes fastest.
Arguments:
- amplitudes: float32 [4096, 32768], P('pair'), may hold values from -6 to 6
- integrals: float32 [32768, 1536], P(('pair', 'rep')), may hold values from -0.375 to 0.375
- row_irrep: int32 [4096], replicated, may hold values from 0 to 7, as said below
- pair_irrep: int32 [32768], P(('pair', 'rep')), may hold values from 0 to 7, as said below
- slab_irrep: int32 [1536], replicated, may hold values from 0 to 7, as said below
Outputs:
- ladder: float32 [4096, 1536], P('pair', 'rep')
The draws below stay inside these ranges and needn't reach their ends.
Inputs may be any that keep to these rules, and one draw needn't show every extreme that they name: `row_irrep`: irrep labels are non-decreasing within each aligned block of 64 occupied pairs: contiguous symmetry blocks of varying size. `pair_irrep`: irrep labels are non-decreasing within each aligned block of 128 virtual pairs: contiguous symmetry blocks of varying size. `slab_irrep`: irrep labels are non-decreasing within each aligned block of 1536 // 4 slab pairs: contiguous symmetry blocks of varying size.
All inputs are finite; a program needn't handle non-finite values.
Results may differ from the reference program's by a relative error of at most 0.0003.
Values sent between devices are 32-bit elements; how exact they have to be, the bound alone decides.
No kernel may reach another device: no remote copies, remote signals or barrier semaphores. Data moves between devices by JAX's collectives and lax.ppermute only.
A program may use at most 128 MiB of HBM per device.

```python
import jax
import jax.numpy as jnp
from jax import lax

ROW_DEV = 64
AB_DEV = 128
CD = 1536
IRREPS = 8
ROWS = 4096
AB = 32768
N_PAIR = 64
N_REP = 4


def sorted_labels(key, total, block):
    labels = jax.random.randint(key, (total,), 0, IRREPS)
    return jnp.sort(labels.reshape(total // block, block), axis=1).reshape(total).astype(jnp.int32)


def draw_row_irrep(key, part):
    key = jax.random.fold_in(key, 11)
    return sorted_labels(key, ROWS, ROW_DEV)


def draw_pair_irrep(key, part):
    key = jax.random.fold_in(key, 23)
    return sorted_labels(key, AB, AB_DEV)


def draw_slab_irrep(key, part):
    key = jax.random.fold_in(key, 37)
    return sorted_labels(key, CD, CD // N_REP)


def raised(values, rng, source, target, blocks, factor):
    def block_of(axis_at):
        return (jnp.arange(values.shape[axis_at]) // (values.shape[axis_at] // blocks)).reshape((-1,) + (1,) * (values.ndim - 1 - axis_at))

    one_side = jax.random.permutation(rng, blocks)[block_of(target)]
    far = (block_of(target) + blocks // 2) % blocks
    return jnp.where((block_of(source) == one_side) | (block_of(source) == far), factor * values, values)


def block_scale(rng, extent, shards, low, largest):
    gain, own = 1.0, jax.random.fold_in(rng, 6)
    for axis_at, blocks in shards:
        draws = jnp.exp(jax.random.uniform(jax.random.fold_in(own, axis_at), (blocks,), jnp.float32, low / len(shards), largest / len(shards)))
        gain = gain * jnp.repeat(draws, extent[axis_at] // blocks).reshape([-1 if axis == axis_at else 1 for axis in range(len(extent))])
    return gain


def scatter_about(own_key, dims, spread, reach, cuts=(), held_as=jnp.bfloat16):
    loudness = block_scale(own_key, dims, cuts, -0.22, 0.18) if cuts else 1.0
    drawn = jax.random.normal(own_key, dims, jnp.float32) * spread * loudness
    return jnp.minimum(jnp.maximum(drawn, -reach), reach).astype(held_as)


def gaussian_with(stream_key, dims, spread, bound, split, heavy, dtype=jnp.bfloat16):
    values = spread * jax.random.normal(stream_key, dims, jnp.float32)
    if split:
        values = values * block_scale(stream_key, dims, split, -0.22, 0.18)
    return jnp.clip(raised(values, jax.random.fold_in(stream_key, 3), *heavy), -bound, bound).astype(dtype)


def setup_inputs(seed: int = 0) -> dict:
    streams_of = jax.random.split(jax.random.key(seed), 6)
    amplitudes = scatter_about(streams_of[0], (ROWS, AB), 1.0, 6.0, ((0, 64),), jnp.float32)
    integrals = gaussian_with(streams_of[1], (AB, CD), (AB // 8) ** -0.5, 0.375, ((0, 256),), (0, 1, 256, 6.0), jnp.float32)
    row_irrep = draw_row_irrep(jax.random.fold_in(streams_of[5], 71), 0)
    pair_irrep = draw_pair_irrep(jax.random.fold_in(streams_of[5], 71), 0)
    slab_irrep = draw_slab_irrep(jax.random.fold_in(streams_of[5], 71), 0)
    return dict(amplitudes=amplitudes, integrals=integrals, row_irrep=row_irrep, pair_irrep=pair_irrep, slab_irrep=slab_irrep)


def reference(amplitudes, integrals, row_irrep, pair_irrep, slab_irrep):
    kept_integrals = jnp.where(pair_irrep[:, None] == slab_irrep[None, :], integrals, jnp.zeros_like(integrals))
    row_blocks = amplitudes.reshape(N_PAIR, ROW_DEV, AB)
    label_blocks = row_irrep.reshape(N_PAIR, ROW_DEV)

    def block_product(pieces):
        rows_block, labels_block = pieces
        kept_rows = jnp.where(labels_block[:, None] == pair_irrep[None, :], rows_block, jnp.zeros_like(rows_block))
        return jnp.dot(kept_rows, kept_integrals, precision=lax.Precision.HIGHEST, preferred_element_type=jnp.float32)

    result = lax.map(block_product, (row_blocks, label_blocks))
    return result.reshape(ROWS, CD)
```

```python
import functools

import jax
import jax.numpy as jnp
from jax import lax
from jax.experimental import pallas as pl
from jax.experimental.pallas import tpu as pltpu
from jax.sharding import Mesh
from jax.sharding import PartitionSpec as P

Z, Y, C, X = 8, 4, 2, 4
IRREPS = 8
ROW_DEV = 64
AB_DEV = 128
CD = 1536
CD_DEV = CD // X
WIDTH = 240
SLOTS = WIDTH - 1
BLOCKS = Z * C
AB_GROUP = BLOCKS * AB_DEV
SHIFTS = (1, Y - 1, 2)
VMEM = pl.BlockSpec(memory_space=pltpu.VMEM)
SMEM = pl.BlockSpec(memory_space=pltpu.SMEM)
ANY = pl.BlockSpec(memory_space=pl.ANY)
PARAMS = pltpu.CompilerParams(vmem_limit_bytes=40 * 2**20)
NT = (((1,), (1,)), ((), ()))
NN = (((1,), (0,)), ((), ()))


def split(value):
    high = value.astype(jnp.bfloat16)
    low = (value - high.astype(jnp.float32)).astype(jnp.bfloat16)
    return high, low


def one_hot(rank, offset):
    slot = lax.broadcasted_iota(jnp.int32, (WIDTH, rank.shape[1]), 0)
    hit = (slot == rank - offset) & (slot < SLOTS)
    return jnp.where(hit, 1.0, 0.0).astype(jnp.bfloat16)


def label_column(row):
    return jnp.broadcast_to(row, (128, 128)).T


def rank_kernel(slab_ref, rank_ref, rounds_ref):
    slab = slab_ref[...]
    mine = slab == lax.broadcasted_iota(jnp.int32, (IRREPS, CD), 0)
    lane = lax.broadcasted_iota(jnp.int32, (IRREPS, CD), 1)
    count = mine.astype(jnp.int32)
    shift = 1
    while shift < CD:
        count = count + jnp.where(lane >= shift, pltpu.roll(count, shift, 1), 0)
        shift *= 2
    rank_ref[...] = jnp.sum(jnp.where(mine, count, 0), axis=0, keepdims=True) - 1
    rounds_ref[0] = lax.div(jnp.max(count) + (SLOTS - 1), SLOTS)


def compact_kernel(round_ref, integrals_ref, pair_ref, slab_ref, rank_ref, out_ref):
    labels = label_column(pair_ref[...].astype(jnp.float32))
    slab = slab_ref[...].astype(jnp.float32)
    kept = jnp.concatenate(
        [
            jnp.where(labels == slab[:, at : at + 128], integrals_ref[:, at : at + 128], 0.0)
            for at in range(0, CD, 128)
        ],
        axis=1,
    )
    high, low = split(kept)
    chosen = one_hot(rank_ref[...], round_ref[0] * SLOTS)
    packed = lax.dot_general(chosen, high, NT, preferred_element_type=jnp.float32)
    packed += lax.dot_general(chosen, low, NT, preferred_element_type=jnp.float32)
    slot = lax.broadcasted_iota(jnp.int32, (WIDTH, AB_DEV), 0)
    out_ref[...] = jnp.where(slot == SLOTS, pair_ref[...].astype(jnp.float32), packed)


def select_kernel(at_ref, amplitudes_ref, *refs):
    outs, sems = refs[:-1], refs[-1]
    y, x = at_ref[1], at_ref[3]
    copies = []
    for d, shift in enumerate(SHIFTS):
        target = lax.rem(y + shift, Y)
        for block in range(BLOCKS):
            z, c = divmod(block, C)
            source = pl.multiple_of((((z * Y + target) * C + c) * X + x) * AB_DEV, AB_DEV)
            copy = pltpu.make_async_copy(
                amplitudes_ref.at[:, pl.ds(source, AB_DEV)],
                outs[d].at[:, pl.ds(block * AB_DEV, AB_DEV)],
                sems.at[d, block],
            )
            copy.start()
            copies.append(copy)
    for copy in copies:
        copy.wait()


def product_kernel(at_ref, amplitudes_ref, *refs):
    arrived = refs[:3]
    blocks = refs[3 : 3 + BLOCKS]
    rows_ref = refs[3 + BLOCKS]
    outs = refs[4 + BLOCKS : 8 + BLOCKS]
    own, thigh, tlow, vhigh, vlow, sems = refs[8 + BLOCKS :]
    z, y, c, x = at_ref[0], at_ref[1], at_ref[2], at_ref[3]
    copies = []
    for block in range(BLOCKS):
        bz, bc = divmod(block, C)
        source = pl.multiple_of((((bz * Y + y) * C + bc) * X + x) * AB_DEV, AB_DEV)
        copy = pltpu.make_async_copy(
            amplitudes_ref.at[:, pl.ds(source, AB_DEV)],
            own.at[:, pl.ds(block * AB_DEV, AB_DEV)],
            sems.at[block],
        )
        copy.start()
        copies.append(copy)
    columns = []
    for k, block in enumerate(blocks):
        value = block[...]
        at = pl.ds(k * AB_DEV, AB_DEV)
        high, low = split(value)
        vhigh[:, at] = high
        vlow[:, at] = low
        columns.append(value[SLOTS : SLOTS + 1, :])
    for copy in copies:
        copy.wait()
    for d, (ref, shift) in enumerate(zip((own,) + tuple(arrived), (0,) + SHIFTS)):
        source = lax.rem(y - shift + Y, Y)
        both = label_column(rows_ref[pl.ds(z * Y + source, 1), :].astype(jnp.float32))
        labels = jnp.where(c == 0, both[:ROW_DEV], both[ROW_DEV:])
        for k in range(BLOCKS):
            steps, other = divmod(k, C)
            bz = lax.rem(z + steps, Z)
            bc = lax.rem(c + other, C)
            at = pl.ds(pl.multiple_of((bz * C + bc) * AB_DEV, AB_DEV), AB_DEV)
            kept = jnp.where(labels == columns[k], ref[:, at], 0.0)
            high, low = split(kept)
            thigh[d * ROW_DEV : (d + 1) * ROW_DEV, k * AB_DEV : (k + 1) * AB_DEV] = high
            tlow[d * ROW_DEV : (d + 1) * ROW_DEV, k * AB_DEV : (k + 1) * AB_DEV] = low
    total = lax.dot_general(thigh[...], vhigh[...], NT, preferred_element_type=jnp.float32)
    total += lax.dot_general(thigh[...], vlow[...], NT, preferred_element_type=jnp.float32)
    total += lax.dot_general(tlow[...], vhigh[...], NT, preferred_element_type=jnp.float32)
    for d, out in enumerate(outs):
        out[...] = total[d * ROW_DEV : (d + 1) * ROW_DEV]


def sum_kernel(a_ref, b_ref, c_ref, d_ref, out_ref):
    out_ref[...] = (a_ref[...] + b_ref[...]) + (c_ref[...] + d_ref[...])


def expand_kernel(round_ref, at_ref, a_ref, b_ref, c_ref, d_ref, rows_ref, slab_ref, rank_ref, out_ref):
    z, y, c, x = at_ref[0], at_ref[1], at_ref[2], at_ref[3]
    total = (a_ref[...] + b_ref[...]) + (c_ref[...] + d_ref[...])
    at = pl.ds(pl.multiple_of(x * CD_DEV, CD_DEV), CD_DEV)
    chosen = one_hot(rank_ref[:, at], round_ref[0] * SLOTS)
    high = total.astype(jnp.bfloat16)
    rest = total - high.astype(jnp.float32)
    middle, low = split(rest)
    wide = lax.dot_general(high, chosen, NN, preferred_element_type=jnp.float32)
    wide += lax.dot_general(middle, chosen, NN, preferred_element_type=jnp.float32)
    wide += lax.dot_general(low, chosen, NN, preferred_element_type=jnp.float32)
    both = label_column(rows_ref[pl.ds(z * Y + y, 1), :].astype(jnp.float32))
    labels = jnp.where(c == 0, both[:ROW_DEV], both[ROW_DEV:])
    slab = slab_ref[:, at].astype(jnp.float32)
    for k in range(0, CD_DEV, 128):
        out_ref[:, k : k + 128] = jnp.where(labels == slab[:, k : k + 128], wide[:, k : k + 128], 0.0)


def shifted(value, axis, by):
    size = {"z": Z, "y": Y, "c": C, "x": X}[axis]
    return lax.ppermute(value, axis, [(i, (i + by) % size) for i in range(size)])


def f32(*shape):
    return jax.ShapeDtypeStruct(shape, jnp.float32)


def per_device(amplitudes, integrals, row_irrep, pair_irrep, slab_irrep):
    at = jnp.stack([lax.axis_index(a) for a in ("z", "y", "c", "x")]).astype(jnp.int32)
    rows = row_irrep.reshape(-1, 128)
    pair = pair_irrep.reshape(1, AB_DEV)
    slab = slab_irrep.reshape(1, CD)
    rank, rounds = pl.pallas_call(
        rank_kernel,
        out_shape=(jax.ShapeDtypeStruct((1, CD), jnp.int32), jax.ShapeDtypeStruct((1,), jnp.int32)),
        in_specs=[VMEM],
        out_specs=(VMEM, SMEM),
        name="rank",
    )(slab)

    pieces = pl.pallas_call(
        select_kernel,
        out_shape=[f32(ROW_DEV, AB_GROUP)] * 3,
        in_specs=[SMEM, ANY],
        out_specs=[ANY] * 3,
        scratch_shapes=[pltpu.SemaphoreType.DMA((3, BLOCKS))],
        name="select",
    )(at, amplitudes)
    arrived = [shifted(piece, "y", shift) for piece, shift in zip(pieces, SHIFTS)]

    def ladder_round(number):
        number = number.reshape(1)
        packed = pl.pallas_call(
            compact_kernel,
            out_shape=f32(WIDTH, AB_DEV),
            in_specs=[SMEM, VMEM, VMEM, VMEM, VMEM],
            out_specs=VMEM,
            compiler_params=PARAMS,
            name="compact",
        )(number, integrals, pair, slab, rank)
        blocks = {0: packed}
        up = down = packed
        for step in range(1, Z // 2 + 1):
            up = shifted(up, "z", -1)
            blocks[step] = up
            if step < Z // 2:
                down = shifted(down, "z", 1)
                blocks[Z - step] = down
        gathered = []
        for step in range(Z):
            gathered += [blocks[step], shifted(blocks[step], "c", 1)]
        parts = pl.pallas_call(
            product_kernel,
            out_shape=[f32(ROW_DEV, WIDTH)] * 4,
            in_specs=[SMEM, ANY] + [VMEM] * (4 + BLOCKS),
            out_specs=[VMEM] * 4,
            scratch_shapes=[
                pltpu.VMEM((ROW_DEV, AB_GROUP), jnp.float32),
                pltpu.VMEM((Y * ROW_DEV, AB_GROUP), jnp.bfloat16),
                pltpu.VMEM((Y * ROW_DEV, AB_GROUP), jnp.bfloat16),
                pltpu.VMEM((WIDTH, AB_GROUP), jnp.bfloat16),
                pltpu.VMEM((WIDTH, AB_GROUP), jnp.bfloat16),
                pltpu.SemaphoreType.DMA((BLOCKS,)),
            ],
            compiler_params=PARAMS,
            name="product",
        )(at, amplitudes, *arrived, *gathered, rows)
        back = [shifted(part, "y", -shift) for part, shift in zip(parts[1:], SHIFTS)]
        mine = pl.pallas_call(
            sum_kernel,
            out_shape=f32(ROW_DEV, WIDTH),
            in_specs=[VMEM] * 4,
            out_specs=VMEM,
            name="sum",
        )(parts[0], *back)
        others = [shifted(mine, "x", shift) for shift in (1, X - 1, 2)]
        return pl.pallas_call(
            expand_kernel,
            out_shape=f32(ROW_DEV, CD_DEV),
            in_specs=[SMEM, SMEM] + [VMEM] * 7,
            out_specs=VMEM,
            compiler_params=PARAMS,
            name="expand",
        )(number, at, mine, *others, rows, slab, rank)

    first = ladder_round(jnp.zeros((), jnp.int32))
    _, ladder = lax.while_loop(
        lambda state: state[0] < rounds[0],
        lambda state: (state[0] + 1, state[1] + ladder_round(state[0])),
        (jnp.ones((), jnp.int32), first),
    )
    return ladder


def solution(mesh):
    grid = Mesh(mesh.devices.reshape(Z, Y, C, X), ("z", "y", "c", "x"))
    placed = (P(("z", "y", "c"), None), P(("z", "y", "c", "x"), None), P(), P(("z", "y", "c", "x")), P())
    return jax.shard_map(
        per_device, mesh=grid, in_specs=placed, out_specs=P(("z", "y", "c"), "x"), check_vma=False
    )
```

```python
import jax
import jax.numpy as jnp
from jax import lax
from jax.experimental import pallas as pl
from jax.experimental.pallas import tpu as pltpu
from jax.sharding import Mesh
from jax.sharding import PartitionSpec as P

Z, Y, C, X = 8, 4, 2, 4
IRREPS = 8
ROW_DEV = 64
AB_DEV = 128
CD = 1536
CD_DEV = CD // X
LANES = 128
CHUNKS = CD // LANES
CHUNKS_DEV = CD_DEV // LANES
SLOTS = 72
LABEL = X * SLOTS
WIDTH = LABEL + 8
BLOCKS = Z * C
AB_GROUP = BLOCKS * AB_DEV
SHIFTS = (0, 1, Y - 1, 2)
VMEM = pl.BlockSpec(memory_space=pltpu.VMEM)
SMEM = pl.BlockSpec(memory_space=pltpu.SMEM)
ANY = pl.BlockSpec(memory_space=pl.ANY)
PARAMS = pltpu.CompilerParams(vmem_limit_bytes=24 * 2**20)
WHOLE = pltpu.CompilerParams(vmem_limit_bytes=58 * 2**20)
NT = (((1,), (1,)), ((), ()))
NN = (((1,), (0,)), ((), ()))


def split(value):
    high = value.astype(jnp.bfloat16)
    low = (value - high.astype(jnp.float32)).astype(jnp.bfloat16)
    return high, low


def place():
    return [lax.axis_index(axis) for axis in ("z", "y", "c", "x")]


def one_hot(rank, offset):
    slot = lax.broadcasted_iota(jnp.int32, (SLOTS, rank.shape[1]), 0)
    return jnp.where(slot == rank - offset, 1.0, 0.0).astype(jnp.bfloat16)


def label_column(row):
    return jnp.broadcast_to(row.astype(jnp.float32), (LANES, LANES)).T


def find_ranks(slab_ref, rank_ref):
    kinds = lax.broadcasted_iota(jnp.int32, (IRREPS, LANES), 0)
    mine = [slab_ref[k : k + 1, :] == kinds for k in range(CHUNKS)]
    ones = jnp.concatenate([jnp.where(m, 1.0, 0.0) for m in mine], axis=0).astype(jnp.bfloat16)
    row = lax.broadcasted_iota(jnp.int32, (LANES, 2 * LANES), 0)
    column = lax.broadcasted_iota(jnp.int32, (LANES, 2 * LANES), 1)
    upper = jnp.where(row <= column, 1.0, 0.0).astype(jnp.bfloat16)
    counts = lax.dot_general(ones, upper, NN, preferred_element_type=jnp.float32)
    most = jnp.zeros((IRREPS, LANES), jnp.float32)
    for k in range(CHUNKS):
        if k % CHUNKS_DEV == 0:
            before = jnp.zeros((IRREPS, LANES), jnp.float32)
        count = counts[k * IRREPS : (k + 1) * IRREPS]
        place_in = jnp.where(mine[k], before + count[:, :LANES], 0.0)
        rank_ref[k : k + 1, :] = jnp.sum(place_in, axis=0, keepdims=True).astype(jnp.int32) - 1
        before = before + count[:, LANES:]
        most = jnp.maximum(most, before)
    return jnp.max(most).astype(jnp.int32)


def compact(offset, integrals_ref, pair_ref, slab_ref, rank_ref, out_ref):
    labels = label_column(pair_ref[...])
    for q in range(X):
        kept, chosen = [], []
        for k in range(q * CHUNKS_DEV, (q + 1) * CHUNKS_DEV):
            slab = slab_ref[k : k + 1, :].astype(jnp.float32)
            value = integrals_ref[:, k * LANES : (k + 1) * LANES]
            kept.append(jnp.where(labels == slab, value, 0.0))
            chosen.append(one_hot(rank_ref[k : k + 1, :], offset))
        high, low = split(jnp.concatenate(kept, axis=1))
        chosen = jnp.concatenate(chosen, axis=1)
        packed = lax.dot_general(chosen, high, NT, preferred_element_type=jnp.float32)
        packed += lax.dot_general(chosen, low, NT, preferred_element_type=jnp.float32)
        out_ref[q * SLOTS : (q + 1) * SLOTS, :] = packed
    out_ref[LABEL:WIDTH, :] = jnp.broadcast_to(pair_ref[...].astype(jnp.float32), (8, LANES))


def own_columns(amplitudes_ref, out_ref, sems, target, first=0):
    x = lax.axis_index("x")
    copies = []
    for block in range(out_ref.shape[1] // AB_DEV):
        bz, bc = divmod(first + block, C)
        source = pl.multiple_of((((bz * Y + target) * C + bc) * X + x) * AB_DEV, AB_DEV)
        copy = pltpu.make_async_copy(
            amplitudes_ref.at[:, pl.ds(source, AB_DEV)],
            out_ref.at[:, pl.ds(block * AB_DEV, AB_DEV)],
            sems.at[block],
        )
        copy.start()
        copies.append(copy)
    return copies


def select_kernel(amplitudes_ref, up_ref, down_ref, own_ref, sems):
    y = lax.axis_index("y")
    far, near, half = pl.ds(AB_GROUP, AB_GROUP // 2), pl.ds(0, AB_GROUP), BLOCKS // 2
    copies = own_columns(amplitudes_ref, up_ref.at[:, near], sems.at[0], lax.rem(y + 1, Y))
    copies += own_columns(amplitudes_ref, down_ref.at[:, near], sems.at[1], lax.rem(y + Y - 1, Y))
    copies += own_columns(amplitudes_ref, up_ref.at[:, far], sems.at[2], lax.rem(y + 2, Y))
    copies += own_columns(amplitudes_ref, down_ref.at[:, far], sems.at[3], lax.rem(y + 2, Y), half)
    copies += own_columns(amplitudes_ref, own_ref, sems.at[4], y)
    for copy in copies:
        copy.wait()


def compact_kernel(round_ref, integrals_ref, pair_ref, slab_ref, out_ref, rank_ref, rounds_ref):
    most = find_ranks(slab_ref, rank_ref)
    rounds_ref[0] = lax.div(most + (SLOTS - 1), SLOTS)
    compact(round_ref[0] * SLOTS, integrals_ref, pair_ref, slab_ref, rank_ref, out_ref)


def split_kernel(own_ref, up_ref, down_ref, far_up_ref, far_down_ref, high_ref, low_ref):
    half = AB_GROUP // 2
    for d, ref in enumerate((own_ref, up_ref, down_ref)):
        row = pl.ds(d * ROW_DEV, ROW_DEV)
        high_ref[row, :], low_ref[row, :] = split(ref[:, :AB_GROUP])
    row = pl.ds(3 * ROW_DEV, ROW_DEV)
    high_ref[row, :half], low_ref[row, :half] = split(far_up_ref[...])
    high_ref[row, half:], low_ref[row, half:] = split(far_down_ref[...])


def row_labels(rows_ref, z, y, c):
    both = label_column(rows_ref[pl.ds(z * Y + y, 1), :])
    return jnp.where(c == 0, both[:ROW_DEV], both[ROW_DEV:])


def masked_product(high_ref, low_ref, blocks, other, rows_ref, thigh, tlow, vhigh, vlow):
    z, y, c, x = place()
    core = lax.rem(c + other, C)
    columns = []
    for k, block in enumerate(blocks):
        at = pl.ds(k * AB_DEV, AB_DEV)
        for q in range(X):
            high, low = split(block[q * SLOTS : (q + 1) * SLOTS, :])
            vhigh[q * LANES : q * LANES + SLOTS, at] = high
            vlow[q * LANES : q * LANES + SLOTS, at] = low
        columns.append(block[LABEL : LABEL + 1, :])
    for d, shift in enumerate(SHIFTS):
        labels = row_labels(rows_ref, z, lax.rem(y - shift + Y, Y), c)
        rows = pl.ds(d * ROW_DEV, ROW_DEV)
        for k in range(Z):
            at = pl.ds(pl.multiple_of((lax.rem(z + k, Z) * C + core) * AB_DEV, AB_DEV), AB_DEV)
            to = pl.ds(k * AB_DEV, AB_DEV)
            mask = jnp.where(labels == columns[k], 1.0, 0.0).astype(jnp.bfloat16)
            thigh[rows, to] = high_ref[rows, at] * mask
            tlow[rows, to] = low_ref[rows, at] * mask
    total = lax.dot_general(thigh[...], vhigh[...], NT, preferred_element_type=jnp.float32)
    total += lax.dot_general(thigh[...], vlow[...], NT, preferred_element_type=jnp.float32)
    total += lax.dot_general(tlow[...], vhigh[...], NT, preferred_element_type=jnp.float32)
    return total


def own_product_kernel(high_ref, low_ref, *refs):
    blocks = refs[:Z]
    rows_ref, out_ref, *scratch = refs[Z:]
    out_ref[...] = masked_product(high_ref, low_ref, blocks, 0, rows_ref, *scratch)


def product_kernel(high_ref, low_ref, *refs):
    blocks = refs[:Z]
    rows_ref, sum_ref, out_ref, *scratch = refs[Z:]
    z, y, c, x = place()
    total = sum_ref[...] + masked_product(high_ref, low_ref, blocks, 1, rows_ref, *scratch)
    for d, shift in enumerate(SHIFTS):
        target = lax.rem(y - shift + Y, Y)
        for q in range(X):
            out_ref[target * X + q] = total[d * ROW_DEV : (d + 1) * ROW_DEV, q * LANES : q * LANES + SLOTS]


def expand_kernel(round_ref, parts_ref, rows_ref, slab_ref, rank_ref, out_ref):
    z, y, c, x = place()
    total = parts_ref[0]
    for k in range(1, Y * X):
        total += parts_ref[k]
    high = total.astype(jnp.bfloat16)
    middle, low = split(total - high.astype(jnp.float32))
    labels = row_labels(rows_ref, z, y, c)
    for k in range(CHUNKS_DEV):
        at = pl.ds(x * CHUNKS_DEV + k, 1)
        chosen = one_hot(rank_ref[at, :], round_ref[0] * SLOTS)
        wide = lax.dot_general(high, chosen, NN, preferred_element_type=jnp.float32)
        wide += lax.dot_general(middle, chosen, NN, preferred_element_type=jnp.float32)
        wide += lax.dot_general(low, chosen, NN, preferred_element_type=jnp.float32)
        slab = slab_ref[at, :].astype(jnp.float32)
        out_ref[:, k * LANES : (k + 1) * LANES] = jnp.where(labels == slab, wide, 0.0)


def shifted(value, axis, by):
    size = {"z": Z, "y": Y, "c": C, "x": X}[axis]
    return lax.ppermute(value, axis, [(i, (i + by) % size) for i in range(size)])


def f32(*shape):
    return jax.ShapeDtypeStruct(shape, jnp.float32)


def i32(*shape):
    return jax.ShapeDtypeStruct(shape, jnp.int32)


def per_device(amplitudes, integrals, row_irrep, pair_irrep, slab_irrep):
    rows = row_irrep.reshape(-1, LANES)
    pair = pair_irrep.reshape(1, AB_DEV)
    slab = slab_irrep.reshape(CHUNKS, LANES)
    *pieces, own = pl.pallas_call(
        select_kernel,
        out_shape=[f32(ROW_DEV, AB_GROUP * 3 // 2)] * 2 + [f32(ROW_DEV, AB_GROUP)],
        in_specs=[ANY],
        out_specs=[VMEM] * 3,
        scratch_shapes=[pltpu.SemaphoreType.DMA((Y + 1, BLOCKS))],
        compiler_params=WHOLE,
        name="select",
    )(amplitudes)
    near = [shifted(piece, "y", shift) for piece, shift in zip(pieces, (1, -1))]
    far = [shifted(piece[:, AB_GROUP:], "y", shift) for piece, shift in zip(near, (1, -1))]
    halves = pl.pallas_call(
        split_kernel,
        out_shape=[jax.ShapeDtypeStruct((Y * ROW_DEV, AB_GROUP), jnp.bfloat16)] * 2,
        in_specs=[VMEM] * 5,
        out_specs=[VMEM] * 2,
        compiler_params=PARAMS,
        name="split",
    )(own, *near, *far)

    def pack(number):
        return pl.pallas_call(
            compact_kernel,
            out_shape=[f32(WIDTH, AB_DEV), i32(CHUNKS, LANES), i32(1)],
            in_specs=[SMEM] + [VMEM] * 3,
            out_specs=[VMEM, VMEM, SMEM],
            compiler_params=PARAMS,
            name="compact",
        )(number.reshape(1), integrals, pair, slab)

    def ladder_round(number, packed, rank):
        blocks = {0: packed}
        up = down = packed
        for step in range(1, Z // 2 + 1):
            up = shifted(up, "z", -1)
            blocks[step] = up
            if step < Z // 2:
                down = shifted(down, "z", 1)
                blocks[Z - step] = down
        scratch = [
            pltpu.VMEM((Y * ROW_DEV, Z * AB_DEV), jnp.bfloat16),
            pltpu.VMEM((Y * ROW_DEV, Z * AB_DEV), jnp.bfloat16),
            pltpu.VMEM((X * LANES, Z * AB_DEV), jnp.bfloat16),
            pltpu.VMEM((X * LANES, Z * AB_DEV), jnp.bfloat16),
        ]
        blocks = [blocks[step] for step in range(Z)]
        others = [shifted(block, "c", 1) for block in blocks]
        partial = pl.pallas_call(
            own_product_kernel,
            out_shape=f32(Y * ROW_DEV, X * LANES),
            in_specs=[VMEM] * (2 + Z + 1),
            out_specs=VMEM,
            scratch_shapes=scratch,
            compiler_params=PARAMS,
            name="own_product",
        )(*halves, *blocks, rows)
        parts = pl.pallas_call(
            product_kernel,
            out_shape=f32(Y * X, ROW_DEV, SLOTS),
            in_specs=[VMEM] * (4 + Z),
            out_specs=VMEM,
            scratch_shapes=scratch,
            compiler_params=PARAMS,
            name="product",
        )(*halves, *others, rows, partial)
        parts = lax.all_to_all(parts, ("y", "x"), split_axis=0, concat_axis=0, tiled=True)
        return pl.pallas_call(
            expand_kernel,
            out_shape=f32(ROW_DEV, CD_DEV),
            in_specs=[SMEM] + [VMEM] * 4,
            out_specs=VMEM,
            compiler_params=PARAMS,
            name="expand",
        )(number.reshape(1), parts, rows, slab, rank)

    def extra_round(state):
        number, ladder = state
        packed, rank, _ = pack(number)
        return number + 1, ladder + ladder_round(number, packed, rank)

    number = jnp.zeros((), jnp.int32)
    packed, rank, rounds = pack(number)
    first = ladder_round(number, packed, rank)
    _, ladder = lax.while_loop(lambda state: state[0] < rounds[0], extra_round, (number + 1, first))
    return ladder


def solution(mesh):
    grid = Mesh(mesh.devices.reshape(Z, Y, C, X), ("z", "y", "c", "x"))
    placed = (P(("z", "y", "c"), None), P(("z", "y", "c", "x"), None), P(), P(("z", "y", "c", "x")), P())
    return jax.shard_map(
        per_device, mesh=grid, in_specs=placed, out_specs=P(("z", "y", "c"), "x"), check_vma=False
    )
```

```python
import jax
import jax.numpy as jnp
from jax import lax
from jax.experimental import pallas as pl
from jax.experimental.pallas import tpu as pltpu
from jax.sharding import Mesh
from jax.sharding import PartitionSpec as P

Z, Y, C, X = 8, 4, 2, 4
IRREPS = 8
ROW_DEV = 64
AB_DEV = 128
CD = 1536
CD_DEV = CD // X
LANES = 128
CHUNKS = CD // LANES
CHUNKS_DEV = CD_DEV // LANES
SLOTS = 72
FOLD = 40
LABEL = X * SLOTS
WIDTH = LABEL + 8
BLOCKS = Z * C
AB_GROUP = BLOCKS * AB_DEV
SHIFTS = (0, 1, Y - 1, 2)
VMEM = pl.BlockSpec(memory_space=pltpu.VMEM)
SMEM = pl.BlockSpec(memory_space=pltpu.SMEM)
ANY = pl.BlockSpec(memory_space=pl.ANY)
PARAMS = pltpu.CompilerParams(vmem_limit_bytes=24 * 2**20)
WHOLE = pltpu.CompilerParams(vmem_limit_bytes=58 * 2**20)
NT = (((1,), (1,)), ((), ()))
NN = (((1,), (0,)), ((), ()))
TN = (((0,), (0,)), ((), ()))


def split(value):
    high = value.astype(jnp.bfloat16)
    low = (value - high.astype(jnp.float32)).astype(jnp.bfloat16)
    return high, low


def place():
    return [lax.axis_index(axis) for axis in ("z", "y", "c", "x")]


def one_hot(rank, offset):
    slot = lax.broadcasted_iota(jnp.int32, (SLOTS, rank.shape[1]), 0)
    return jnp.where(slot == rank - offset, 1.0, 0.0).astype(jnp.bfloat16)


def label_column(row):
    return jnp.broadcast_to(row.astype(jnp.float32), (LANES, LANES)).T


def find_ranks(slab_ref, rank_ref):
    kinds = lax.broadcasted_iota(jnp.int32, (IRREPS, LANES), 0)
    mine = [slab_ref[k : k + 1, :] == kinds for k in range(CHUNKS)]
    ones = jnp.concatenate([jnp.where(m, 1.0, 0.0) for m in mine], axis=0).astype(jnp.bfloat16)
    row = lax.broadcasted_iota(jnp.int32, (LANES, 2 * LANES), 0)
    column = lax.broadcasted_iota(jnp.int32, (LANES, 2 * LANES), 1)
    upper = jnp.where(row <= column, 1.0, 0.0).astype(jnp.bfloat16)
    counts = lax.dot_general(ones, upper, NN, preferred_element_type=jnp.float32)
    most = jnp.zeros((IRREPS, LANES), jnp.float32)
    for k in range(CHUNKS):
        if k % CHUNKS_DEV == 0:
            before = jnp.zeros((IRREPS, LANES), jnp.float32)
        count = counts[k * IRREPS : (k + 1) * IRREPS]
        place_in = jnp.where(mine[k], before + count[:, :LANES], 0.0)
        rank_ref[k : k + 1, :] = jnp.sum(place_in, axis=0, keepdims=True).astype(jnp.int32) - 1
        before = before + count[:, LANES:]
        most = jnp.maximum(most, before)
    return jnp.max(most).astype(jnp.int32)


def compact(offset, integrals_ref, pair_ref, slab_ref, rank_ref, out_ref):
    labels = label_column(pair_ref[...])
    for q in range(X):
        kept, chosen = [], []
        for k in range(q * CHUNKS_DEV, (q + 1) * CHUNKS_DEV):
            slab = slab_ref[k : k + 1, :].astype(jnp.float32)
            value = integrals_ref[:, k * LANES : (k + 1) * LANES]
            kept.append(jnp.where(labels == slab, value, 0.0))
            chosen.append(one_hot(rank_ref[k : k + 1, :], offset))
        high, low = split(jnp.concatenate(kept, axis=1))
        chosen = jnp.concatenate(chosen, axis=1)
        packed = lax.dot_general(chosen, high, NT, preferred_element_type=jnp.float32)
        packed += lax.dot_general(chosen, low, NT, preferred_element_type=jnp.float32)
        out_ref[q * SLOTS : (q + 1) * SLOTS, :] = packed
    out_ref[LABEL:WIDTH, :] = jnp.broadcast_to(pair_ref[...].astype(jnp.float32), (8, LANES))


def own_columns(amplitudes_ref, out_ref, sems, target, first=0):
    x = lax.axis_index("x")
    copies = []
    for block in range(out_ref.shape[1] // AB_DEV):
        bz, bc = divmod(first + block, C)
        source = pl.multiple_of((((bz * Y + target) * C + bc) * X + x) * AB_DEV, AB_DEV)
        copy = pltpu.make_async_copy(
            amplitudes_ref.at[:, pl.ds(source, AB_DEV)],
            out_ref.at[:, pl.ds(block * AB_DEV, AB_DEV)],
            sems.at[block],
        )
        copy.start()
        copies.append(copy)
    return copies


def select_kernel(amplitudes_ref, up_ref, down_ref, own_ref, sems):
    y = lax.axis_index("y")
    far, near, half = pl.ds(AB_GROUP, AB_GROUP // 2), pl.ds(0, AB_GROUP), BLOCKS // 2
    copies = own_columns(amplitudes_ref, up_ref.at[:, near], sems.at[0], lax.rem(y + 1, Y))
    copies += own_columns(amplitudes_ref, down_ref.at[:, near], sems.at[1], lax.rem(y + Y - 1, Y))
    copies += own_columns(amplitudes_ref, up_ref.at[:, far], sems.at[2], lax.rem(y + 2, Y))
    copies += own_columns(amplitudes_ref, down_ref.at[:, far], sems.at[3], lax.rem(y + 2, Y), half)
    copies += own_columns(amplitudes_ref, own_ref, sems.at[4], y)
    for copy in copies:
        copy.wait()


def compact_kernel(round_ref, integrals_ref, pair_ref, slab_ref, out_ref, rank_ref, rounds_ref):
    most = find_ranks(slab_ref, rank_ref)
    rounds_ref[0] = lax.div(most + (SLOTS - 1), SLOTS)
    compact(round_ref[0] * SLOTS, integrals_ref, pair_ref, slab_ref, rank_ref, out_ref)


def split_kernel(own_ref, up_ref, down_ref, far_up_ref, far_down_ref, high_ref, low_ref, own, sem):
    copy = pltpu.make_async_copy(own_ref, own, sem)
    copy.start()
    half = AB_GROUP // 2
    for d, ref in ((1, up_ref), (2, down_ref)):
        row = pl.ds(d * ROW_DEV, ROW_DEV)
        high_ref[row, :], low_ref[row, :] = split(ref[:, :AB_GROUP])
    row = pl.ds(3 * ROW_DEV, ROW_DEV)
    high_ref[row, :half], low_ref[row, :half] = split(far_up_ref[...])
    high_ref[row, half:], low_ref[row, half:] = split(far_down_ref[...])
    copy.wait()
    row = pl.ds(0, ROW_DEV)
    high_ref[row, :], low_ref[row, :] = split(own[...])


def row_labels(rows_ref, z, y, c):
    both = label_column(rows_ref[pl.ds(z * Y + y, 1), :])
    return jnp.where(c == 0, both[:ROW_DEV], both[ROW_DEV:])


def masked_product(high_ref, low_ref, blocks, other, rows_ref, thigh, tlow, vhigh, vlow):
    z, y, c, x = place()
    core = lax.rem(c + other, C)
    columns = []
    for k, block in enumerate(blocks):
        at = pl.ds(k * AB_DEV, AB_DEV)
        vhigh[:, at], vlow[:, at] = split(block[:LABEL, :])
        columns.append(block[LABEL : LABEL + 1, :])
    for d, shift in enumerate(SHIFTS):
        labels = row_labels(rows_ref, z, lax.rem(y - shift + Y, Y), c)
        rows = pl.ds(d * ROW_DEV, ROW_DEV)
        for k in range(Z):
            at = pl.ds(pl.multiple_of((lax.rem(z + k, Z) * C + core) * AB_DEV, AB_DEV), AB_DEV)
            to = pl.ds(k * AB_DEV, AB_DEV)
            mask = jnp.where(labels == columns[k], 1.0, 0.0).astype(jnp.bfloat16)
            thigh[rows, to] = high_ref[rows, at] * mask
            tlow[rows, to] = low_ref[rows, at] * mask
    total = lax.dot_general(vhigh[...], thigh[...], NT, preferred_element_type=jnp.float32)
    total += lax.dot_general(vlow[...], thigh[...], NT, preferred_element_type=jnp.float32)
    total += lax.dot_general(vhigh[...], tlow[...], NT, preferred_element_type=jnp.float32)
    return total


def own_product_kernel(high_ref, low_ref, *refs):
    blocks = refs[:Z]
    rows_ref, out_ref, *scratch = refs[Z:]
    out_ref[...] = masked_product(high_ref, low_ref, blocks, 0, rows_ref, *scratch)


def product_kernel(high_ref, low_ref, *refs):
    blocks = refs[:Z]
    rows_ref, sum_ref, out_ref, *scratch = refs[Z:]
    z, y, c, x = place()
    total = sum_ref[...] + masked_product(high_ref, low_ref, blocks, 1, rows_ref, *scratch)
    for d, shift in enumerate(SHIFTS):
        target = lax.rem(y - shift + Y, Y)
        for q in range(X):
            piece = total[q * SLOTS : (q + 1) * SLOTS, d * ROW_DEV : (d + 1) * ROW_DEV]
            rest = jnp.concatenate([piece[FOLD:], jnp.zeros((2 * FOLD - SLOTS, ROW_DEV), jnp.float32)], axis=0)
            out_ref[target * X + q] = jnp.concatenate([piece[:FOLD], rest], axis=1)


def expand_kernel(round_ref, parts_ref, rows_ref, slab_ref, rank_ref, out_ref):
    z, y, c, x = place()
    total = parts_ref[0]
    for k in range(1, Y * X):
        total += parts_ref[k]
    total = jnp.concatenate([total[:, :ROW_DEV], total[: SLOTS - FOLD, ROW_DEV:]], axis=0)
    high = total.astype(jnp.bfloat16)
    middle, low = split(total - high.astype(jnp.float32))
    labels = row_labels(rows_ref, z, y, c)
    for k in range(CHUNKS_DEV):
        at = pl.ds(x * CHUNKS_DEV + k, 1)
        to = pl.ds(k * LANES, LANES)
        chosen = one_hot(rank_ref[at, :], round_ref[0] * SLOTS)
        wide = lax.dot_general(high, chosen, TN, preferred_element_type=jnp.float32)
        wide += lax.dot_general(middle, chosen, TN, preferred_element_type=jnp.float32)
        wide += lax.dot_general(low, chosen, TN, preferred_element_type=jnp.float32)
        slab = slab_ref[at, :].astype(jnp.float32)
        out_ref[:, to] = jnp.where(labels == slab, wide, 0.0)


def shifted(value, axis, by):
    size = {"z": Z, "y": Y, "c": C, "x": X}[axis]
    return lax.ppermute(value, axis, [(i, (i + by) % size) for i in range(size)])


def f32(*shape):
    return jax.ShapeDtypeStruct(shape, jnp.float32)


def i32(*shape):
    return jax.ShapeDtypeStruct(shape, jnp.int32)


def per_device(amplitudes, integrals, row_irrep, pair_irrep, slab_irrep):
    rows = row_irrep.reshape(-1, LANES)
    pair = pair_irrep.reshape(1, AB_DEV)
    slab = slab_irrep.reshape(CHUNKS, LANES)
    *pieces, own = pl.pallas_call(
        select_kernel,
        out_shape=[f32(ROW_DEV, AB_GROUP * 3 // 2)] * 2 + [f32(ROW_DEV, AB_GROUP)],
        in_specs=[ANY],
        out_specs=[VMEM] * 3,
        scratch_shapes=[pltpu.SemaphoreType.DMA((Y + 1, BLOCKS))],
        compiler_params=WHOLE,
        name="select",
    )(amplitudes)
    def pack(number):
        return pl.pallas_call(
            compact_kernel,
            out_shape=[f32(WIDTH, AB_DEV), i32(CHUNKS, LANES), i32(1)],
            in_specs=[SMEM] + [VMEM] * 3,
            out_specs=[VMEM, VMEM, SMEM],
            compiler_params=PARAMS,
            name="compact",
        )(number.reshape(1), integrals, pair, slab)

    def gather(packed):
        blocks = {0: packed}
        up = down = packed
        for step in range(1, Z // 2 + 1):
            up = shifted(up, "z", -1)
            blocks[step] = up
            if step < Z // 2:
                down = shifted(down, "z", 1)
                blocks[Z - step] = down
        return [blocks[step] for step in range(Z)]

    def ladder_round(number, blocks, rank):
        others = [shifted(block, "c", 1) for block in blocks]
        scratch = [
            pltpu.VMEM((Y * ROW_DEV, Z * AB_DEV), jnp.bfloat16),
            pltpu.VMEM((Y * ROW_DEV, Z * AB_DEV), jnp.bfloat16),
            pltpu.VMEM((LABEL, Z * AB_DEV), jnp.bfloat16),
            pltpu.VMEM((LABEL, Z * AB_DEV), jnp.bfloat16),
        ]
        partial = pl.pallas_call(
            own_product_kernel,
            out_shape=f32(LABEL, Y * ROW_DEV),
            in_specs=[VMEM] * (2 + Z + 1),
            out_specs=VMEM,
            scratch_shapes=scratch,
            compiler_params=PARAMS,
            name="own_product",
        )(*halves, *blocks, rows)
        parts = pl.pallas_call(
            product_kernel,
            out_shape=f32(Y * X, FOLD, 2 * ROW_DEV),
            in_specs=[VMEM] * (4 + Z),
            out_specs=VMEM,
            scratch_shapes=scratch,
            compiler_params=PARAMS,
            name="product",
        )(*halves, *others, rows, partial)
        parts = lax.all_to_all(parts, ("y", "x"), split_axis=0, concat_axis=0, tiled=True)
        return pl.pallas_call(
            expand_kernel,
            out_shape=f32(ROW_DEV, CD_DEV),
            in_specs=[SMEM] + [VMEM] * 4,
            out_specs=VMEM,
            compiler_params=PARAMS,
            name="expand",
        )(number.reshape(1), parts, rows, slab, rank)

    def extra_round(state):
        number, base = state
        packed, rank, _ = pack(number)
        return number + 1, base + ladder_round(number, gather(packed), rank)

    number = jnp.zeros((), jnp.int32)
    packed, rank, rounds = pack(number)
    blocks = gather(packed)
    near = [shifted(piece, "y", shift) for piece, shift in zip(pieces, (1, -1))]
    forward = near
    far = [shifted(piece[:, AB_GROUP:], "y", shift) for piece, shift in zip(forward, (1, -1))]
    halves = pl.pallas_call(
        split_kernel,
        out_shape=[jax.ShapeDtypeStruct((Y * ROW_DEV, AB_GROUP), jnp.bfloat16)] * 2,
        in_specs=[ANY] + [VMEM] * 4,
        out_specs=[VMEM] * 2,
        scratch_shapes=[pltpu.VMEM((ROW_DEV, AB_GROUP), jnp.float32), pltpu.SemaphoreType.DMA],
        compiler_params=PARAMS,
        name="split",
    )(own, *near, *far)


    first = ladder_round(number, blocks, rank)
    _, ladder = lax.while_loop(lambda state: state[0] < rounds[0], extra_round, (number + 1, first))
    return ladder


def solution(mesh):
    grid = Mesh(mesh.devices.reshape(Z, Y, C, X), ("z", "y", "c", "x"))
    placed = (P(("z", "y", "c"), None), P(("z", "y", "c", "x"), None), P(), P(("z", "y", "c", "x")), P())
    return jax.shard_map(
        per_device, mesh=grid, in_specs=placed, out_specs=P(("z", "y", "c"), "x"), check_vma=False
    )
```

```python
import jax
import jax.numpy as jnp
from jax import lax
from jax.experimental import pallas as pl
from jax.experimental.pallas import tpu as pltpu
from jax.sharding import Mesh
from jax.sharding import PartitionSpec as P

Z, Y, C, X = 8, 4, 2, 4
IRREPS = 8
ROW_DEV = 64
AB_DEV = 128
CD = 1536
CD_DEV = CD // X
LANES = 128
CHUNKS = CD // LANES
CHUNKS_DEV = CD_DEV // LANES
SLOTS = 72
FOLD = 40
LABEL = X * SLOTS
WIDTH = LABEL + 8
BLOCKS = Z * C
AB_GROUP = BLOCKS * AB_DEV
SHIFTS = (0, 1, Y - 1, 2)
VMEM = pl.BlockSpec(memory_space=pltpu.VMEM)
SMEM = pl.BlockSpec(memory_space=pltpu.SMEM)
ANY = pl.BlockSpec(memory_space=pl.ANY)
PARAMS = pltpu.CompilerParams(vmem_limit_bytes=24 * 2**20)
WHOLE = pltpu.CompilerParams(vmem_limit_bytes=58 * 2**20)
NT = (((1,), (1,)), ((), ()))
NN = (((1,), (0,)), ((), ()))
TN = (((0,), (0,)), ((), ()))


def split(value):
    high = value.astype(jnp.bfloat16)
    low = (value - high.astype(jnp.float32)).astype(jnp.bfloat16)
    return high, low


def place():
    return [lax.axis_index(axis) for axis in ("z", "y", "c", "x")]


def one_hot(rank, offset):
    slot = lax.broadcasted_iota(jnp.int32, (SLOTS, rank.shape[1]), 0)
    return jnp.where(slot == rank - offset, 1.0, 0.0).astype(jnp.bfloat16)


def label_column(row):
    return jnp.broadcast_to(row.astype(jnp.float32), (LANES, LANES)).T


def find_ranks(slab_ref, rank_ref):
    kinds = lax.broadcasted_iota(jnp.int32, (IRREPS, LANES), 0)
    mine = [slab_ref[k : k + 1, :] == kinds for k in range(CHUNKS)]
    ones = jnp.concatenate([jnp.where(m, 1.0, 0.0) for m in mine], axis=0).astype(jnp.bfloat16)
    row = lax.broadcasted_iota(jnp.int32, (LANES, 2 * LANES), 0)
    column = lax.broadcasted_iota(jnp.int32, (LANES, 2 * LANES), 1)
    upper = jnp.where(row <= column, 1.0, 0.0).astype(jnp.bfloat16)
    counts = lax.dot_general(ones, upper, NN, preferred_element_type=jnp.float32)
    most = jnp.zeros((IRREPS, LANES), jnp.float32)
    for k in range(CHUNKS):
        if k % CHUNKS_DEV == 0:
            before = jnp.zeros((IRREPS, LANES), jnp.float32)
        count = counts[k * IRREPS : (k + 1) * IRREPS]
        place_in = jnp.where(mine[k], before + count[:, :LANES], 0.0)
        rank_ref[k : k + 1, :] = jnp.sum(place_in, axis=0, keepdims=True).astype(jnp.int32) - 1
        before = before + count[:, LANES:]
        most = jnp.maximum(most, before)
    return jnp.max(most).astype(jnp.int32)


def compact(offset, integrals_ref, pair_ref, slab_ref, rank_ref, out_ref):
    labels = label_column(pair_ref[...])
    for q in range(X):
        kept, chosen = [], []
        for k in range(q * CHUNKS_DEV, (q + 1) * CHUNKS_DEV):
            slab = slab_ref[k : k + 1, :].astype(jnp.float32)
            value = integrals_ref[:, k * LANES : (k + 1) * LANES]
            kept.append(jnp.where(labels == slab, value, 0.0))
            chosen.append(one_hot(rank_ref[k : k + 1, :], offset))
        high, low = split(jnp.concatenate(kept, axis=1))
        chosen = jnp.concatenate(chosen, axis=1)
        packed = lax.dot_general(chosen, high, NT, preferred_element_type=jnp.float32)
        packed += lax.dot_general(chosen, low, NT, preferred_element_type=jnp.float32)
        out_ref[q * SLOTS : (q + 1) * SLOTS, :] = packed
    out_ref[LABEL:WIDTH, :] = jnp.broadcast_to(pair_ref[...].astype(jnp.float32), (8, LANES))


def own_columns(amplitudes_ref, out_ref, sems, target, first=0):
    x = lax.axis_index("x")
    copies = []
    for block in range(out_ref.shape[1] // AB_DEV):
        bz, bc = divmod(first + block, C)
        source = pl.multiple_of((((bz * Y + target) * C + bc) * X + x) * AB_DEV, AB_DEV)
        copy = pltpu.make_async_copy(
            amplitudes_ref.at[:, pl.ds(source, AB_DEV)],
            out_ref.at[:, pl.ds(block * AB_DEV, AB_DEV)],
            sems.at[block],
        )
        copy.start()
        copies.append(copy)
    return copies


def select_kernel(amplitudes_ref, up_ref, down_ref, own_ref, sems):
    y = lax.axis_index("y")
    far, near, half = pl.ds(AB_GROUP, AB_GROUP // 2), pl.ds(0, AB_GROUP), BLOCKS // 2
    copies = own_columns(amplitudes_ref, up_ref.at[:, near], sems.at[0], lax.rem(y + 1, Y))
    copies += own_columns(amplitudes_ref, down_ref.at[:, near], sems.at[1], lax.rem(y + Y - 1, Y))
    copies += own_columns(amplitudes_ref, up_ref.at[:, far], sems.at[2], lax.rem(y + 2, Y))
    copies += own_columns(amplitudes_ref, down_ref.at[:, far], sems.at[3], lax.rem(y + 2, Y), half)
    copies += own_columns(amplitudes_ref, own_ref, sems.at[4], y)
    for copy in copies:
        copy.wait()


def compact_kernel(round_ref, integrals_ref, pair_ref, slab_ref, out_ref, rank_ref, rounds_ref):
    most = find_ranks(slab_ref, rank_ref)
    rounds_ref[0] = lax.div(most + (SLOTS - 1), SLOTS)
    compact(round_ref[0] * SLOTS, integrals_ref, pair_ref, slab_ref, rank_ref, out_ref)


def own_split_kernel(own_ref, high_ref, low_ref):
    high_ref[...], low_ref[...] = split(own_ref[...])


def split_kernel(up_ref, down_ref, far_up_ref, far_down_ref, high_ref, low_ref):
    half = AB_GROUP // 2
    for d, ref in enumerate((up_ref, down_ref)):
        row = pl.ds(d * ROW_DEV, ROW_DEV)
        high_ref[row, :], low_ref[row, :] = split(ref[:, :AB_GROUP])
    row = pl.ds(2 * ROW_DEV, ROW_DEV)
    high_ref[row, :half], low_ref[row, :half] = split(far_up_ref[...])
    high_ref[row, half:], low_ref[row, half:] = split(far_down_ref[...])


def row_labels(rows_ref, z, y, c):
    both = label_column(rows_ref[pl.ds(z * Y + y, 1), :])
    return jnp.where(c == 0, both[:ROW_DEV], both[ROW_DEV:])


def masked_product(halves, blocks, other, rows_ref, thigh, tlow, vhigh, vlow):
    z, y, c, x = place()
    core = lax.rem(c + other, C)
    columns = []
    for k, block in enumerate(blocks):
        at = pl.ds(k * AB_DEV, AB_DEV)
        vhigh[:, at], vlow[:, at] = split(block[:LABEL, :])
        columns.append(block[LABEL : LABEL + 1, :])
    for d, shift in enumerate(SHIFTS):
        labels = row_labels(rows_ref, z, lax.rem(y - shift + Y, Y), c)
        rows = pl.ds(d * ROW_DEV, ROW_DEV)
        high_ref, low_ref = halves[:2] if d == 0 else halves[2:]
        source = pl.ds(max(d - 1, 0) * ROW_DEV, ROW_DEV)
        for k in range(Z):
            at = pl.ds(pl.multiple_of((lax.rem(z + k, Z) * C + core) * AB_DEV, AB_DEV), AB_DEV)
            to = pl.ds(k * AB_DEV, AB_DEV)
            mask = jnp.where(labels == columns[k], 1.0, 0.0).astype(jnp.bfloat16)
            thigh[rows, to] = high_ref[source, at] * mask
            tlow[rows, to] = low_ref[source, at] * mask
    total = lax.dot_general(vhigh[...], thigh[...], NT, preferred_element_type=jnp.float32)
    total += lax.dot_general(vlow[...], thigh[...], NT, preferred_element_type=jnp.float32)
    total += lax.dot_general(vhigh[...], tlow[...], NT, preferred_element_type=jnp.float32)
    return total


def own_product_kernel(*refs):
    halves, refs = refs[:4], refs[4:]
    blocks = refs[:Z]
    rows_ref, out_ref, *scratch = refs[Z:]
    out_ref[...] = masked_product(halves, blocks, 0, rows_ref, *scratch)


def product_kernel(*refs):
    halves, refs = refs[:4], refs[4:]
    blocks = refs[:Z]
    rows_ref, sum_ref, out_ref, *scratch = refs[Z:]
    z, y, c, x = place()
    total = sum_ref[...] + masked_product(halves, blocks, 1, rows_ref, *scratch)
    for d, shift in enumerate(SHIFTS):
        target = lax.rem(y - shift + Y, Y)
        for q in range(X):
            piece = total[q * SLOTS : (q + 1) * SLOTS, d * ROW_DEV : (d + 1) * ROW_DEV]
            rest = jnp.concatenate([piece[FOLD:], jnp.zeros((2 * FOLD - SLOTS, ROW_DEV), jnp.float32)], axis=0)
            out_ref[target * X + q] = jnp.concatenate([piece[:FOLD], rest], axis=1)


def expand_kernel(round_ref, parts_ref, rows_ref, slab_ref, rank_ref, out_ref):
    z, y, c, x = place()
    total = parts_ref[0]
    for k in range(1, Y * X):
        total += parts_ref[k]
    total = jnp.concatenate([total[:, :ROW_DEV], total[: SLOTS - FOLD, ROW_DEV:]], axis=0)
    high = total.astype(jnp.bfloat16)
    middle, low = split(total - high.astype(jnp.float32))
    labels = row_labels(rows_ref, z, y, c)
    for k in range(CHUNKS_DEV):
        at = pl.ds(x * CHUNKS_DEV + k, 1)
        to = pl.ds(k * LANES, LANES)
        chosen = one_hot(rank_ref[at, :], round_ref[0] * SLOTS)
        wide = lax.dot_general(high, chosen, TN, preferred_element_type=jnp.float32)
        wide += lax.dot_general(middle, chosen, TN, preferred_element_type=jnp.float32)
        wide += lax.dot_general(low, chosen, TN, preferred_element_type=jnp.float32)
        slab = slab_ref[at, :].astype(jnp.float32)
        out_ref[:, to] = jnp.where(labels == slab, wide, 0.0)


def shifted(value, axis, by):
    size = {"z": Z, "y": Y, "c": C, "x": X}[axis]
    return lax.ppermute(value, axis, [(i, (i + by) % size) for i in range(size)])


def f32(*shape):
    return jax.ShapeDtypeStruct(shape, jnp.float32)


def i32(*shape):
    return jax.ShapeDtypeStruct(shape, jnp.int32)


def per_device(amplitudes, integrals, row_irrep, pair_irrep, slab_irrep):
    rows = row_irrep.reshape(-1, LANES)
    pair = pair_irrep.reshape(1, AB_DEV)
    slab = slab_irrep.reshape(CHUNKS, LANES)
    *pieces, own = pl.pallas_call(
        select_kernel,
        out_shape=[f32(ROW_DEV, AB_GROUP * 3 // 2)] * 2 + [f32(ROW_DEV, AB_GROUP)],
        in_specs=[ANY],
        out_specs=[VMEM] * 3,
        scratch_shapes=[pltpu.SemaphoreType.DMA((Y + 1, BLOCKS))],
        compiler_params=WHOLE,
        name="select",
    )(amplitudes)
    def pack(number):
        return pl.pallas_call(
            compact_kernel,
            out_shape=[f32(WIDTH, AB_DEV), i32(CHUNKS, LANES), i32(1)],
            in_specs=[SMEM] + [VMEM] * 3,
            out_specs=[VMEM, VMEM, SMEM],
            compiler_params=PARAMS,
            name="compact",
        )(number.reshape(1), integrals, pair, slab)

    def gather(packed):
        blocks = {0: packed}
        up = down = packed
        for step in range(1, Z // 2 + 1):
            up = shifted(up, "z", -1)
            blocks[step] = up
            if step < Z // 2:
                down = shifted(down, "z", 1)
                blocks[Z - step] = down
        return [blocks[step] for step in range(Z)]

    def ladder_round(number, blocks, rank):
        others = [shifted(block, "c", 1) for block in blocks]
        scratch = [
            pltpu.VMEM((Y * ROW_DEV, Z * AB_DEV), jnp.bfloat16),
            pltpu.VMEM((Y * ROW_DEV, Z * AB_DEV), jnp.bfloat16),
            pltpu.VMEM((LABEL, Z * AB_DEV), jnp.bfloat16),
            pltpu.VMEM((LABEL, Z * AB_DEV), jnp.bfloat16),
        ]
        partial = pl.pallas_call(
            own_product_kernel,
            out_shape=f32(LABEL, Y * ROW_DEV),
            in_specs=[VMEM] * (4 + Z + 1),
            out_specs=VMEM,
            scratch_shapes=scratch,
            compiler_params=PARAMS,
            name="own_product",
        )(*halves, *blocks, rows)
        parts = pl.pallas_call(
            product_kernel,
            out_shape=f32(Y * X, FOLD, 2 * ROW_DEV),
            in_specs=[VMEM] * (6 + Z),
            out_specs=VMEM,
            scratch_shapes=scratch,
            compiler_params=PARAMS,
            name="product",
        )(*halves, *others, rows, partial)
        parts = lax.all_to_all(parts, ("y", "x"), split_axis=0, concat_axis=0, tiled=True)
        return pl.pallas_call(
            expand_kernel,
            out_shape=f32(ROW_DEV, CD_DEV),
            in_specs=[SMEM] + [VMEM] * 4,
            out_specs=VMEM,
            compiler_params=PARAMS,
            name="expand",
        )(number.reshape(1), parts, rows, slab, rank)

    def extra_round(state):
        number, base = state
        packed, rank, _ = pack(number)
        return number + 1, base + ladder_round(number, gather(packed), rank)

    number = jnp.zeros((), jnp.int32)
    packed, rank, rounds = pack(number)
    own_halves = pl.pallas_call(
        own_split_kernel,
        out_shape=[jax.ShapeDtypeStruct((ROW_DEV, AB_GROUP), jnp.bfloat16)] * 2,
        in_specs=[VMEM],
        out_specs=[VMEM] * 2,
        compiler_params=PARAMS,
        name="own_split",
    )(own)
    own_halves, packed = lax.optimization_barrier((list(own_halves), packed))
    blocks = gather(packed)
    near = [shifted(piece, "y", shift) for piece, shift in zip(pieces, (1, -1))]
    forward = near
    far = [shifted(piece[:, AB_GROUP:], "y", shift) for piece, shift in zip(forward, (1, -1))]
    halves = pl.pallas_call(
        split_kernel,
        out_shape=[jax.ShapeDtypeStruct((3 * ROW_DEV, AB_GROUP), jnp.bfloat16)] * 2,
        in_specs=[VMEM] * 4,
        out_specs=[VMEM] * 2,
        compiler_params=PARAMS,
        name="split",
    )(*near, *far)
    halves = [*own_halves, *halves]


    first = ladder_round(number, blocks, rank)
    _, ladder = lax.while_loop(lambda state: state[0] < rounds[0], extra_round, (number + 1, first))
    return ladder


def solution(mesh):
    grid = Mesh(mesh.devices.reshape(Z, Y, C, X), ("z", "y", "c", "x"))
    placed = (P(("z", "y", "c"), None), P(("z", "y", "c", "x"), None), P(), P(("z", "y", "c", "x")), P())
    return jax.shard_map(
        per_device, mesh=grid, in_specs=placed, out_specs=P(("z", "y", "c"), "x"), check_vma=False
    )
```
